32 devices in a mesh: dp: 16 (over z, x, core), tensor: 2 (over y).
Axes of the slice: x: 2, y: 2, z: 4, core: 2. Of those that a mesh axis runs over, the one named last changes fastest.
Arguments:
- quant_rows: int32 [4096, 2048], P(('dp', 'tensor')), may hold values from -127 to 127
- residual: bfloat16 [4096, 2048], P(('dp', 'tensor')), may hold values from -48 to 48
- row_scale: float32 [4096], P(('dp', 'tensor')), may hold values from 0.004 to 0.04
- norm_gain: float32 [2048], replicated, may hold values from 0.1 to 1.9
- gate_pre: bfloat16 [4096, 7168], P('dp', 'tensor'), may hold values from -6 to 6
- up_pre: bfloat16 [4096, 7168], P('dp', 'tensor'), may hold values from -6 to 6
- hidden_grad: bfloat16 [4096, 7168], P('dp', 'tensor'), may hold values from -6 to 6
- gate_weight: bfloat16 [2048, 7168], P('dp', 'tensor'), may hold values from -0.125 to 0.125
- up_weight: bfloat16 [2048, 7168], P('dp', 'tensor'), may hold values from -0.125 to 0.125
Outputs:
- resid_grad: bfloat16 [4096, 2048], P(('dp', 'tensor'))
- gate_weight_grad: float32 [2048, 7168], P('dp', 'tensor')
- up_weight_grad: float32 [2048, 7168], P('dp', 'tensor')
The draws below stay inside these ranges and needn't reach their ends.
All inputs are finite; a program needn't handle non-finite values.
Results may differ from the reference program's by a relative error of at most 0.014.
Values may be sent and summed in bfloat16 or wider, within the bound.
A program may use at most 128 MiB of HBM per device.

```python
import math
import jax
import jax.numpy as jnp
from jax import lax

D = 2048
FF = 7168
TOK_DEV = 128
TOKENS = 4096
N_DP = 16
N_TENSOR = 2


def draw_residual(key, part):
    first_key, second_key, third_key = jax.random.split(jax.random.fold_in(key, 7), 3)
    row_scales = jnp.exp(jax.random.uniform(first_key, (TOKENS, 1), jnp.float32, math.log(0.3), math.log(3.0)))
    column_scales = jnp.exp(jax.random.uniform(second_key, (1, D), jnp.float32, math.log(0.3), math.log(3.0)))
    entries = jnp.clip(jax.random.normal(third_key, (TOKENS, D), jnp.float32), -4.0, 4.0)
    return (entries * row_scales * column_scales).astype(jnp.bfloat16)


def with_ends(result, rng, least, high):
    index_at = [jax.random.randint(jax.random.fold_in(rng, axis), (), 0, length) for axis, length in enumerate(result.shape)]
    widest = result.shape.index(max(result.shape))
    beside = index_at[:widest] + [(index_at[widest] + 1) % result.shape[widest]] + index_at[widest + 1:]
    return result.at[tuple(index_at)].set(least).at[tuple(beside)].set(high)


def shard_levels(key, shape, shards, least, top_value):
    def one(axis_at, parts):
        steps = jax.random.uniform(jax.random.fold_in(jax.random.fold_in(key, 6), axis_at), (parts,), jnp.float32, least / len(shards), top_value / len(shards))
        return jnp.repeat(jnp.exp(steps), shape[axis_at] // parts).reshape((-1,) + (1,) * (len(shape) - axis_at - 1))

    gain = one(*shards[0])
    for cut in shards[1:]:
        gain = gain * one(*cut)
    return gain


def centred(stream_key, shape, scale, reach, cuts=(), kind=jnp.bfloat16):
    result = scale * jax.random.normal(stream_key, shape, jnp.float32)
    if cuts:
        result = result * shard_levels(stream_key, shape, cuts, -0.22, 0.18)
    return jnp.clip(result, -reach, reach).astype(kind)


def setup_inputs(seed: int = 0) -> dict:
    seeds = jax.random.split(jax.random.key(seed), 10)
    quant_rows = with_ends(jax.random.randint(seeds[0], (TOKENS, D), -127, 128), jax.random.fold_in(seeds[0], 1), -127, 127).astype(jnp.int32)
    residual = draw_residual(jax.random.fold_in(seeds[9], 71), 0)
    row_scale = jnp.clip(jnp.exp(math.log(0.04) - 2.30258502 * jax.random.uniform(seeds[2], (TOKENS,), jnp.float32) ** shard_levels(seeds[2], (TOKENS,), ((0, 32),), -0.2, 0.2)), 0.004, 0.04)
    norm_gain = jnp.clip(1.0 + 0.18 * jax.random.normal(seeds[3], (D,), jnp.float32), 0.1, 1.9)
    gate_pre = centred(seeds[4], (TOKENS, FF), 1.0, 6.0, ((0, 16), (1, 2)))
    up_pre = centred(seeds[5], (TOKENS, FF), 1.0, 6.0, ((0, 16), (1, 2)))
    hidden_grad = centred(seeds[6], (TOKENS, FF), 1.0, 6.0, ((0, 16), (1, 2)))
    gate_weight = centred(seeds[7], (D, FF), D ** -0.5, 0.125, ((0, 16), (1, 2)))
    up_weight = centred(seeds[8], (D, FF), D ** -0.5, 0.125, ((0, 16), (1, 2)))
    return {"quant_rows": quant_rows, "residual": residual, "row_scale": row_scale, "norm_gain": norm_gain, "gate_pre": gate_pre, "up_pre": up_pre, "hidden_grad": hidden_grad, "gate_weight": gate_weight, "up_weight": up_weight}


def norm_rows(residual, quant_rows, row_scale, norm_gain):
    summed_in = residual.astype(jnp.float32) + quant_rows.astype(jnp.float32) * row_scale[:, None]
    inverse = lax.rsqrt(lax.optimization_barrier(jnp.mean(summed_in * summed_in, axis=-1, keepdims=True)) + 1e-05)
    unit_rows = summed_in * inverse
    return (unit_rows, inverse, (unit_rows * norm_gain).astype(jnp.bfloat16))

def reference(quant_rows, residual, row_scale, norm_gain, gate_pre, up_pre, hidden_grad, gate_weight, up_weight):
    slab_rows = TOK_DEV * N_TENSOR
    hidden_block = FF // N_TENSOR
    unit_rows, inverse, normed = norm_rows(residual, quant_rows, row_scale, norm_gain)

    def one_slab(carry_pair, slab_index):
        offset = (slab_index * slab_rows).astype(jnp.int32)

        def slab_part(array):
            return lax.dynamic_slice_in_dim(array, offset, slab_rows, 0)
        gate_val = slab_part(gate_pre).astype(jnp.float32)
        up_val = slab_part(up_pre).astype(jnp.float32)
        grad_val = slab_part(hidden_grad).astype(jnp.float32)
        sigmoid_gate = jax.nn.sigmoid(gate_val)
        up_grad = (grad_val * gate_val * sigmoid_gate).astype(jnp.bfloat16)
        gate_grad = (grad_val * up_val * sigmoid_gate * (1.0 + gate_val * (1.0 - sigmoid_gate))).astype(jnp.bfloat16)
        slab_normed = slab_part(normed)
        gate_part = jnp.dot(slab_normed.T, gate_grad, preferred_element_type=jnp.float32)
        up_part = jnp.dot(slab_normed.T, up_grad, preferred_element_type=jnp.float32)
        new_carry = (carry_pair[0] + lax.optimization_barrier(gate_part.astype(jnp.bfloat16)).astype(jnp.float32), carry_pair[1] + lax.optimization_barrier(up_part.astype(jnp.bfloat16)).astype(jnp.float32))
        normed_grad = jnp.zeros((slab_rows, D), jnp.float32)
        for shard_index in range(N_TENSOR):
            first_col = shard_index * hidden_block
            last_col = first_col + hidden_block
            partial_value = jnp.dot(gate_grad[:, first_col:last_col], gate_weight[:, first_col:last_col].T, preferred_element_type=jnp.float32)
            partial_value = partial_value + jnp.dot(up_grad[:, first_col:last_col], up_weight[:, first_col:last_col].T, preferred_element_type=jnp.float32)
            normed_grad = normed_grad + lax.optimization_barrier(partial_value.astype(jnp.bfloat16)).astype(jnp.float32)
        grad_term = norm_gain * normed_grad
        slab_unit = slab_part(unit_rows)
        slab_inverse = slab_part(inverse)
        input_grad = slab_inverse * (grad_term - slab_unit * lax.optimization_barrier(jnp.mean(slab_unit * grad_term, axis=-1, keepdims=True)))
        return (new_carry, input_grad.astype(jnp.bfloat16))
    zeros = jnp.zeros((D, FF), jnp.float32)
    totals, resid_grad = lax.scan(one_slab, (zeros, zeros), jnp.arange(N_DP, dtype=jnp.int32))
    factor = 1.0 / math.sqrt(TOKENS)
    return (resid_grad.reshape(TOKENS, D), totals[0] * factor, totals[1] * factor)
```

```python
import functools
import math

import jax
import jax.numpy as jnp
from jax import lax
from jax.experimental import pallas as pl
from jax.experimental.pallas import tpu as pltpu
from jax.sharding import PartitionSpec as P

MESH = pl.DeviceIdType.MESH
BF16 = jnp.bfloat16
F32 = jnp.float32
CORES = 2


def line_length(dp):
    for length in (4, 2):
        if dp % (length * CORES) == 0:
            return length
    return 1


def chunk_count(width):
    for count in (7, 4, 2):
        if width % (count * 128) == 0:
            return count
    return 1


def fused_kernel(
    dims,
    factor,
    normed_ref,
    gate_ref,
    up_ref,
    hidden_ref,
    gate_w_ref,
    up_w_ref,
    grad_out,
    gate_out,
    up_out,
    acts,
    weights,
    rs_send,
    rs_recv,
    normed_all,
    acc,
    ng_send,
    ng_recv,
    ag_ss,
    ag_rs,
    rs_ss,
    rs_rs,
    gx_ss,
    gx_rs,
    gc_ss,
    gc_rs,
    n_ss,
    n_rs,
    ng_ss,
    ng_rs,
):
    Z, I, NT, NC, CW = dims
    X = I // CORES
    S = I * NT
    slab = gate_ref.shape[0]
    rows = gate_w_ref.shape[0]
    tok = slab // NT
    dp = lax.axis_index("dp")
    y = lax.axis_index("tensor")
    z = lax.div(dp, I)
    i = lax.rem(dp, I)
    x = lax.div(i, CORES)
    c = lax.rem(i, CORES)
    me = i * NT + y
    base = z * I
    partner = (base + x * CORES + (1 - c), y)
    right = (dp + I, y)
    left = (dp - I, y)

    def member(s):
        return (base + lax.div(s, NT), lax.rem(s, NT))

    def across(other):
        return (base + other * CORES + c, y)

    def copy(src, dst, send_sem, recv_sem, device):
        return pltpu.make_async_remote_copy(
            src_ref=src, dst_ref=dst, send_sem=send_sem, recv_sem=recv_sem,
            device_id=device, device_id_type=MESH,
        )

    barrier = pltpu.get_barrier_semaphore()

    @pl.loop(0, S)
    def _(s):
        @pl.when(s != me)
        def _():
            pl.semaphore_signal(barrier, inc=1, device_id=member(s), device_id_type=MESH)

    @pl.when(z < Z - 1)
    def _():
        pl.semaphore_signal(barrier, inc=1, device_id=right, device_id_type=MESH)

    @pl.when(z > 0)
    def _():
        pl.semaphore_signal(barrier, inc=1, device_id=left, device_id_type=MESH)

    @pl.loop(0, NC)
    def _(k):
        columns = pl.ds(pl.multiple_of(k * CW, 128), CW)
        weights[k, 0, z] = gate_w_ref[:, columns]
        weights[k, 1, z] = up_w_ref[:, columns]

    inside = (z > 0) & (z < Z - 1)

    @pl.when(inside)
    def _():
        pl.semaphore_wait(barrier, S + 1)

    @pl.when(jnp.logical_not(inside))
    def _():
        pl.semaphore_wait(barrier, S if Z > 1 else S - 1)

    def ag_right(k, origin):
        block = weights.at[k, :, origin]
        return copy(block, block, ag_ss.at[k, 0, origin], ag_rs.at[k, origin], right)

    def ag_left(k, origin):
        block = weights.at[k, :, origin]
        return copy(block, block, ag_ss.at[k, 1, origin], ag_rs.at[k, origin], left)

    def normed_copy(s, source):
        place = pl.ds(pl.multiple_of(source * tok, 128), tok)
        return copy(
            normed_ref.at[lax.div(s, NT)], normed_all.at[:, place], n_ss.at[s], n_rs.at[source], member(s)
        )

    @pl.loop(0, S)
    def _(s):
        @pl.when(s != me)
        def _():
            normed_copy(s, me).start()

    @pl.loop(0, NC)
    def _(k):
        @pl.when(z < Z - 1)
        def _():
            ag_right(k, z).start()

        @pl.when(z > 0)
        def _():
            ag_left(k, z).start()

    normed_all[:, pl.ds(pl.multiple_of(me * tok, 128), tok)] = normed_ref[i]

    def act_across(k, other, source):
        block = acts.at[k, :, source * CORES + c]
        return copy(block, block, gx_ss.at[k, other], gx_rs.at[k, source], across(other))

    def act_partner(k, source_x, source_c):
        block = acts.at[k, :, source_x * CORES + source_c]
        return copy(block, block, gc_ss.at[k, source_x], gc_rs.at[k, source_x], partner)

    part = 32

    @pl.loop(0, NC)
    def _(k):
        columns = pl.ds(pl.multiple_of(k * CW, 128), CW)

        @pl.loop(0, slab // part)
        def _(r):
            span = pl.ds(pl.multiple_of(r * part, part), part)
            gate_val = gate_ref[span, columns].astype(F32)
            up_val = up_ref[span, columns].astype(F32)
            grad_val = hidden_ref[span, columns].astype(F32)
            sig = 1.0 / (1.0 + jnp.exp(-gate_val))
            scaled = grad_val * sig
            acts[k, 1, i, span] = (scaled * gate_val).astype(BF16)
            acts[k, 0, i, span] = (scaled * up_val * (1.0 + gate_val * (1.0 - sig))).astype(BF16)

        @pl.loop(0, X)
        def _(other):
            @pl.when(other != x)
            def _():
                act_across(k, other, x).start()

        act_partner(k, x, c).start()

    def rs_right(k, d):
        return copy(rs_send.at[k, d], rs_recv.at[k, d], rs_ss.at[k, d], rs_rs.at[k, d], right)

    def rs_left(k, d, slot):
        return copy(rs_send.at[k, d], rs_recv.at[k, slot], rs_ss.at[k, d], rs_rs.at[k, slot], left)

    def add_in(k, d):
        for t in range(2):
            rs_send[k, d, t] = (rs_send[k, d, t].astype(F32) + rs_recv[k, d, t].astype(F32)).astype(BF16)

    @pl.loop(0, S)
    def _(s):
        @pl.when(s != me)
        def _():
            normed_copy(s, s).wait_recv()

    @pl.loop(0, NC + max(Z - 2, 0))
    def _(it):
        @pl.when(it < NC)
        def _():
            @pl.loop(0, X)
            def _(other):
                @pl.when(other != x)
                def _():
                    act_across(it, other, other).wait_recv()
                    act_partner(it, other, c).start()

            @pl.loop(0, X)
            def _(other):
                act_partner(it, other, 1 - c).wait_recv()

            for t in range(2):
                full = jnp.zeros((Z * rows, CW), F32)
                for j in range(I):
                    full = full + jnp.dot(
                        normed_all[:, j * slab : (j + 1) * slab], acts[it, t, j],
                        preferred_element_type=F32,
                    )
                for d in range(Z):
                    rs_send[it, d, t] = full[d * rows : (d + 1) * rows].astype(BF16)

        kr = it - z

        @pl.when((kr >= 0) & (kr < NC) & (z < Z - 1))
        def _():
            for d in range(Z - 1, 0, -1):
                @pl.when(d > z)
                def _():
                    @pl.when(z > 0)
                    def _():
                        rs_right(kr, d).wait_recv()
                        add_in(kr, d)

                    rs_right(kr, d).start()

        kl = it - (Z - 1 - z)

        @pl.when((kl >= 0) & (kl < NC) & (z > 0))
        def _():
            for d in range(Z - 1):
                @pl.when(d < z)
                def _():
                    @pl.when(z < Z - 1)
                    def _():
                        rs_left(kl, d, d).wait_recv()
                        add_in(kl, d)

                    @pl.when(d < z - 1)
                    def _():
                        rs_left(kl, d, d).start()

                    @pl.when(d == z - 1)
                    def _():
                        rs_left(kl, d, Z).start()

        for h in range(1, Z - 1):
            kh = it - h

            @pl.when((kh >= 0) & (kh < NC) & (z >= h) & (z < Z - 1))
            def _():
                ag_right(kh, z - h).wait_recv()
                ag_right(kh, z - h).start()

            @pl.when((kh >= 0) & (kh < NC) & (z + h < Z) & (z > 0))
            def _():
                ag_left(kh, z + h).wait_recv()
                ag_left(kh, z + h).start()

    @pl.loop(0, NC)
    def _(k):
        for o in range(Z):
            @pl.when((z == Z - 1) & (z != o))
            def _():
                ag_left(k, o).wait_recv()

            @pl.when((z == 0) & (z != o))
            def _():
                ag_right(k, o).wait_recv()

    def ng_copy(s, source):
        return copy(ng_send.at[s], ng_recv.at[source], ng_ss.at[s], ng_rs.at[source], member(s))

    @pl.loop(0, I)
    def _(j):
        acc[...] = jnp.zeros_like(acc)

        @pl.loop(0, NC)
        def _(k):
            for t in range(2):
                acc[...] += lax.dot_general(
                    acts[k, t, j], weights[k, t].reshape(Z * rows, CW),
                    (((1,), (1,)), ((), ())), preferred_element_type=F32,
                )

        @pl.loop(0, NT)
        def _(h):
            s = j * NT + h
            ng_send[s] = acc[pl.ds(pl.multiple_of(h * tok, 128), tok), :].astype(BF16)

            @pl.when(s != me)
            def _():
                ng_copy(s, me).start()

    ng_recv[me] = ng_send[me]

    @pl.loop(0, NC)
    def _(k):
        columns = pl.ds(pl.multiple_of(k * CW, 128), CW)
        gate_out[:, columns] = rs_send[k, z, 0].astype(F32) * factor
        up_out[:, columns] = rs_send[k, z, 1].astype(F32) * factor

        @pl.when(z > 0)
        def _():
            rs_right(k, z).wait_recv()
            gate_out[:, columns] += rs_recv[k, z, 0].astype(F32) * factor
            up_out[:, columns] += rs_recv[k, z, 1].astype(F32) * factor

        @pl.when(z < Z - 1)
        def _():
            rs_left(k, z, Z).wait_recv()
            gate_out[:, columns] += rs_recv[k, Z, 0].astype(F32) * factor
            up_out[:, columns] += rs_recv[k, Z, 1].astype(F32) * factor

    @pl.loop(0, S)
    def _(s):
        @pl.when(s != me)
        def _():
            ng_copy(s, s).wait_recv()

    @pl.loop(0, I)
    def _(j):
        total = ng_recv[j * NT].astype(F32)
        for h in range(1, NT):
            total = total + ng_recv[j * NT + h].astype(F32)
        grad_out[j] = total

    @pl.loop(0, S)
    def _(s):
        @pl.when(s != me)
        def _():
            normed_copy(s, me).wait_send()
            ng_copy(s, me).wait_send()

    @pl.loop(0, NC)
    def _(k):
        @pl.loop(0, X)
        def _(other):
            act_partner(k, other, c).wait_send()

            @pl.when(other != x)
            def _():
                act_across(k, other, x).wait_send()

        for d in range(Z):
            @pl.when(d > z)
            def _():
                rs_right(k, d).wait_send()

            @pl.when(d < z)
            def _():
                rs_left(k, d, d).wait_send()

            @pl.when((z < Z - 1) & (d <= z))
            def _():
                ag_right(k, d).wait_send()

            @pl.when((z > 0) & (d >= z))
            def _():
                ag_left(k, d).wait_send()


def fused(dims, factor, normed, gate_pre, up_pre, hidden_grad, gate_weight, up_weight):
    Z, I, NT, NC, CW = dims
    X = I // CORES
    S = I * NT
    slab = gate_pre.shape[0]
    rows, width = gate_weight.shape
    tok = slab // NT
    depth = Z * rows
    dma = pltpu.SemaphoreType.DMA
    vmem = pl.BlockSpec(memory_space=pltpu.VMEM)
    return pl.pallas_call(
        functools.partial(fused_kernel, dims, factor),
        out_shape=(
            jax.ShapeDtypeStruct((I, tok, depth), F32),
            jax.ShapeDtypeStruct((rows, width), F32),
            jax.ShapeDtypeStruct((rows, width), F32),
        ),
        in_specs=[vmem] * 6,
        out_specs=(vmem, vmem, vmem),
        scratch_shapes=[
            pltpu.VMEM((NC, 2, I, slab, CW), BF16),
            pltpu.VMEM((NC, 2, Z, rows, CW), BF16),
            pltpu.VMEM((NC, Z, 2, rows, CW), BF16),
            pltpu.VMEM((NC, Z + 1, 2, rows, CW), BF16),
            pltpu.VMEM((depth, S * tok), BF16),
            pltpu.VMEM((slab, depth), F32),
            pltpu.VMEM((S, tok, depth), BF16),
            pltpu.VMEM((S, tok, depth), BF16),
            dma((NC, 2, Z)),
            dma((NC, Z)),
            dma((NC, Z)),
            dma((NC, Z + 1)),
            dma((NC, X)),
            dma((NC, X)),
            dma((NC, X)),
            dma((NC, X)),
            dma((S,)),
            dma((S,)),
            dma((S,)),
            dma((S,)),
        ],
        compiler_params=pltpu.CompilerParams(
            collective_id=0, has_side_effects=True, vmem_limit_bytes=61 * 1024 * 1024
        ),
        cost_estimate=pl.CostEstimate(
            flops=8 * slab * I * depth * width, bytes_accessed=20 * 1024 * 1024, transcendentals=slab * width
        ),
    )(normed, gate_pre, up_pre, hidden_grad, gate_weight, up_weight)


def body(
    quant_rows,
    residual,
    row_scale,
    norm_gain,
    gate_pre,
    up_pre,
    hidden_grad,
    gate_weight,
    up_weight,
):
    count = lax.axis_size("dp")
    tensor = lax.axis_size("tensor")
    Z = line_length(count)
    I = count // Z
    tok, depth = residual.shape
    rows = gate_weight.shape[0]
    NC = chunk_count(gate_weight.shape[1])
    CW = gate_weight.shape[1] // NC
    summed_in = residual.astype(F32) + quant_rows.astype(F32) * row_scale[:, None]
    inverse = lax.rsqrt(jnp.mean(summed_in * summed_in, axis=-1, keepdims=True) + 1e-05)
    unit_rows = summed_in * inverse
    normed = (unit_rows * norm_gain).astype(BF16)
    blocks = normed.reshape(tok, Z, I, rows).transpose(2, 1, 3, 0).reshape(I, Z * rows, tok)
    factor = 1.0 / math.sqrt(gate_pre.shape[0] * count)
    summed, gate_out, up_out = fused(
        (Z, I, tensor, NC, CW), factor, blocks, gate_pre, up_pre, hidden_grad, gate_weight, up_weight
    )
    normed_grad = summed.reshape(I, tok, Z, rows).transpose(1, 2, 0, 3).reshape(tok, depth)
    grad_term = norm_gain * normed_grad
    input_grad = inverse * (
        grad_term - unit_rows * jnp.mean(unit_rows * grad_term, axis=-1, keepdims=True)
    )
    return (input_grad.astype(BF16), gate_out, up_out)


def solution(mesh):
    placed = (
        P(("dp", "tensor"), None),
        P(("dp", "tensor"), None),
        P(("dp", "tensor")),
        P(),
        P("dp", "tensor"),
        P("dp", "tensor"),
        P("dp", "tensor"),
        P("dp", "tensor"),
        P("dp", "tensor"),
    )
    return jax.shard_map(
        body,
        mesh=mesh,
        in_specs=placed,
        out_specs=(P(("dp", "tensor"), None), P("dp", "tensor"), P("dp", "tensor")),
        check_vma=False,
    )
```

```python
import functools
import math

import jax
import jax.numpy as jnp
from jax import lax
from jax.experimental import pallas as pl
from jax.experimental.pallas import tpu as pltpu
from jax.sharding import PartitionSpec as P

MESH = pl.DeviceIdType.MESH
BF16 = jnp.bfloat16
F32 = jnp.float32
CORES = 2


def line_length(dp):
    for length in (4, 2):
        if dp % (length * CORES) == 0:
            return length
    return 1


def chunk_count(width):
    for count in (7, 4, 2):
        if width % (count * 128) == 0:
            return count
    return 1


def fused_kernel(
    dims,
    factor,
    normed_ref,
    gate_ref,
    up_ref,
    hidden_ref,
    gate_w_ref,
    up_w_ref,
    unit_ref,
    inverse_ref,
    gain_ref,
    grad_out,
    gate_out,
    up_out,
    acts,
    weights,
    rs_send,
    rs_recv,
    normed_all,
    acc,
    ng_send,
    ng_recv,
    terms,
    ag_ss,
    ag_rs,
    rs_ss,
    rs_rs,
    gx_ss,
    gx_rs,
    gc_ss,
    gc_rs,
    n_ss,
    n_rs,
    ng_ss,
    ng_rs,
):
    Z, I, NT, NC, CW = dims
    X = I // CORES
    S = I * NT
    slab = gate_ref.shape[0]
    rows = gate_w_ref.shape[0]
    tok = slab // NT
    dp = lax.axis_index("dp")
    y = lax.axis_index("tensor")
    z = lax.div(dp, I)
    i = lax.rem(dp, I)
    x = lax.div(i, CORES)
    c = lax.rem(i, CORES)
    me = i * NT + y
    base = z * I
    partner = (base + x * CORES + (1 - c), y)
    right = (dp + I, y)
    left = (dp - I, y)

    def member(s):
        return (base + lax.div(s, NT), lax.rem(s, NT))

    def across(other):
        return (base + other * CORES + c, y)

    def copy(src, dst, send_sem, recv_sem, device):
        return pltpu.make_async_remote_copy(
            src_ref=src, dst_ref=dst, send_sem=send_sem, recv_sem=recv_sem,
            device_id=device, device_id_type=MESH,
        )

    barrier = pltpu.get_barrier_semaphore()

    @pl.loop(0, S)
    def _(s):
        @pl.when(s != me)
        def _():
            pl.semaphore_signal(barrier, inc=1, device_id=member(s), device_id_type=MESH)

    @pl.when(z < Z - 1)
    def _():
        pl.semaphore_signal(barrier, inc=1, device_id=right, device_id_type=MESH)

    @pl.when(z > 0)
    def _():
        pl.semaphore_signal(barrier, inc=1, device_id=left, device_id_type=MESH)

    @pl.loop(0, NC)
    def _(k):
        columns = pl.ds(pl.multiple_of(k * CW, 128), CW)
        weights[k, 0, z] = gate_w_ref[:, columns]
        weights[k, 1, z] = up_w_ref[:, columns]

    inside = (z > 0) & (z < Z - 1)

    @pl.when(inside)
    def _():
        pl.semaphore_wait(barrier, S + 1)

    @pl.when(jnp.logical_not(inside))
    def _():
        pl.semaphore_wait(barrier, S if Z > 1 else S - 1)

    def ag_right(k, origin):
        block = weights.at[k, :, origin]
        return copy(block, block, ag_ss.at[k, 0, origin], ag_rs.at[k, origin], right)

    def ag_left(k, origin):
        block = weights.at[k, :, origin]
        return copy(block, block, ag_ss.at[k, 1, origin], ag_rs.at[k, origin], left)

    def normed_copy(s, source):
        place = pl.ds(pl.multiple_of(source * tok, 128), tok)
        return copy(
            normed_ref.at[lax.div(s, NT)], normed_all.at[:, place], n_ss.at[s], n_rs.at[source], member(s)
        )

    @pl.loop(0, S)
    def _(s):
        @pl.when(s != me)
        def _():
            normed_copy(s, me).start()

    @pl.loop(0, NC)
    def _(k):
        @pl.when(z < Z - 1)
        def _():
            ag_right(k, z).start()

        @pl.when(z > 0)
        def _():
            ag_left(k, z).start()

    normed_all[:, pl.ds(pl.multiple_of(me * tok, 128), tok)] = normed_ref[i]

    def act_across(k, other, source):
        block = acts.at[k, :, source * CORES + c]
        return copy(block, block, gx_ss.at[k, other], gx_rs.at[k, source], across(other))

    def act_partner(k, source_x, source_c):
        block = acts.at[k, :, source_x * CORES + source_c]
        return copy(block, block, gc_ss.at[k, source_x], gc_rs.at[k, source_x], partner)

    part = 32

    @pl.loop(0, NC)
    def _(k):
        columns = pl.ds(pl.multiple_of(k * CW, 128), CW)

        @pl.loop(0, slab // part)
        def _(r):
            span = pl.ds(pl.multiple_of(r * part, part), part)
            gate_val = gate_ref[span, columns].astype(F32)
            up_val = up_ref[span, columns].astype(F32)
            grad_val = hidden_ref[span, columns].astype(F32)
            sig = 1.0 / (1.0 + jnp.exp(-gate_val))
            scaled = grad_val * sig
            acts[k, 1, i, span] = (scaled * gate_val).astype(BF16)
            acts[k, 0, i, span] = (scaled * up_val * (1.0 + gate_val * (1.0 - sig))).astype(BF16)

        @pl.loop(0, X)
        def _(other):
            @pl.when(other != x)
            def _():
                act_across(k, other, x).start()

        act_partner(k, x, c).start()

    def rs_right(k, d):
        return copy(rs_send.at[k, d], rs_recv.at[k, d], rs_ss.at[k, d], rs_rs.at[k, d], right)

    def rs_left(k, d, slot):
        return copy(rs_send.at[k, d], rs_recv.at[k, slot], rs_ss.at[k, d], rs_rs.at[k, slot], left)

    def add_in(k, d):
        for t in range(2):
            rs_send[k, d, t] = (rs_send[k, d, t].astype(F32) + rs_recv[k, d, t].astype(F32)).astype(BF16)

    @pl.loop(0, S)
    def _(s):
        @pl.when(s != me)
        def _():
            normed_copy(s, s).wait_recv()

    @pl.loop(0, NC + max(Z - 2, 0))
    def _(it):
        for h in range(1, Z - 1):
            kh = it - h

            @pl.when((kh >= 0) & (kh < NC) & (z >= h) & (z < Z - 1))
            def _():
                ag_right(kh, z - h).wait_recv()
                ag_right(kh, z - h).start()

            @pl.when((kh >= 0) & (kh < NC) & (z + h < Z) & (z > 0))
            def _():
                ag_left(kh, z + h).wait_recv()
                ag_left(kh, z + h).start()

        @pl.when(it < NC)
        def _():
            @pl.loop(0, X)
            def _(other):
                @pl.when(other != x)
                def _():
                    act_across(it, other, other).wait_recv()
                    act_partner(it, other, c).start()

            @pl.loop(0, X)
            def _(other):
                act_partner(it, other, 1 - c).wait_recv()

            for t in range(2):
                full = jnp.zeros((Z * rows, CW), F32)
                for j in range(I):
                    full = full + jnp.dot(
                        normed_all[:, j * slab : (j + 1) * slab], acts[it, t, j],
                        preferred_element_type=F32,
                    )
                for d in range(Z):
                    rs_send[it, d, t] = full[d * rows : (d + 1) * rows].astype(BF16)

            @pl.when((z == 0) & (Z > 1))
            def _():
                for d in range(Z - 1, 0, -1):
                    rs_right(it, d).start()

            @pl.when((z == Z - 1) & (Z > 1))
            def _():
                for d in range(Z - 1):
                    rs_left(it, d, d if d < Z - 2 else Z).start()

    def ng_copy(s, source):
        return copy(ng_send.at[s], ng_recv.at[source], ng_ss.at[s], ng_rs.at[source], member(s))

    def weights_there():
        @pl.loop(0, NC)
        def _(k):
            for o in range(Z):
                @pl.when((z == Z - 1) & (z != o))
                def _():
                    ag_left(k, o).wait_recv()

                @pl.when((z == 0) & (z != o))
                def _():
                    ag_right(k, o).wait_recv()

    def normed_gradient(j):
        acc[...] = jnp.zeros_like(acc)

        @pl.loop(0, NC)
        def _(k):
            for t in range(2):
                acc[...] += lax.dot_general(
                    acts[k, t, j], weights[k, t].reshape(Z * rows, CW),
                    (((1,), (1,)), ((), ())), preferred_element_type=F32,
                )

        @pl.loop(0, NT)
        def _(h):
            s = j * NT + h
            ng_send[s] = acc[pl.ds(pl.multiple_of(h * tok, 128), tok), :].astype(BF16)

            @pl.when(s != me)
            def _():
                ng_copy(s, me).start()

    weights_there()

    @pl.loop(0, max(NC + max(Z - 3, 0), I + 1))
    def _(it):
        kr = it - jnp.maximum(z - 1, 0)

        @pl.when((kr >= 0) & (kr < NC) & (z > 0) & (z < Z - 1))
        def _():
            for d in range(Z - 1, 1, -1):
                @pl.when(d > z)
                def _():
                    rs_right(kr, d).wait_recv()
                    add_in(kr, d)
                    rs_right(kr, d).start()

        kl = it - jnp.maximum(Z - 2 - z, 0)

        @pl.when((kl >= 0) & (kl < NC) & (z > 0) & (z < Z - 1))
        def _():
            for d in range(Z - 2):
                @pl.when(d < z)
                def _():
                    rs_left(kl, d, d).wait_recv()
                    add_in(kl, d)

                    @pl.when(d < z - 1)
                    def _():
                        rs_left(kl, d, d).start()

                    @pl.when(d == z - 1)
                    def _():
                        rs_left(kl, d, Z).start()

        @pl.when((it >= 1) & (it < I + 1))
        def _():
            normed_gradient(it - 1)

    ng_recv[me] = ng_send[me]

    @pl.loop(0, S)
    def _(s):
        @pl.when(s != me)
        def _():
            ng_copy(s, s).wait_recv()

    tally = jnp.zeros((tok, 1), F32)
    for j in range(I):
        total = ng_recv[j * NT].astype(F32)
        for h in range(1, NT):
            total = total + ng_recv[j * NT + h].astype(F32)
        for o in range(Z):
            first = (o * I + j) * rows
            term = gain_ref[:, first : first + rows] * total[:, o * rows : (o + 1) * rows]
            terms[:, first : first + rows] = term
            tally = tally + jnp.sum(unit_ref[:, first : first + rows] * term, axis=-1, keepdims=True)
    mean = tally * (1.0 / (I * Z * rows))
    grad_out[...] = (inverse_ref[...] * (terms[...] - unit_ref[...] * mean)).astype(BF16)

    @pl.loop(0, NC)
    def _(k):
        columns = pl.ds(pl.multiple_of(k * CW, 128), CW)
        gate_out[:, columns] = rs_send[k, z, 0].astype(F32) * factor
        up_out[:, columns] = rs_send[k, z, 1].astype(F32) * factor

        @pl.when(z > 0)
        def _():
            rs_right(k, z).wait_recv()
            gate_out[:, columns] += rs_recv[k, z, 0].astype(F32) * factor
            up_out[:, columns] += rs_recv[k, z, 1].astype(F32) * factor

        @pl.when(z < Z - 1)
        def _():
            rs_left(k, z, Z).wait_recv()
            gate_out[:, columns] += rs_recv[k, Z, 0].astype(F32) * factor
            up_out[:, columns] += rs_recv[k, Z, 1].astype(F32) * factor

    @pl.loop(0, S)
    def _(s):
        @pl.when(s != me)
        def _():
            normed_copy(s, me).wait_send()
            ng_copy(s, me).wait_send()

    @pl.loop(0, NC)
    def _(k):
        @pl.loop(0, X)
        def _(other):
            act_partner(k, other, c).wait_send()

            @pl.when(other != x)
            def _():
                act_across(k, other, x).wait_send()

        for d in range(Z):
            @pl.when(d > z)
            def _():
                rs_right(k, d).wait_send()

            @pl.when(d < z)
            def _():
                rs_left(k, d, d).wait_send()

            @pl.when((z < Z - 1) & (d <= z))
            def _():
                ag_right(k, d).wait_send()

            @pl.when((z > 0) & (d >= z))
            def _():
                ag_left(k, d).wait_send()


def fused(dims, factor, normed, gate_pre, up_pre, hidden_grad, gate_weight, up_weight, unit_rows, inverse, gain):
    Z, I, NT, NC, CW = dims
    X = I // CORES
    S = I * NT
    slab = gate_pre.shape[0]
    rows, width = gate_weight.shape
    tok = slab // NT
    depth = Z * rows
    dma = pltpu.SemaphoreType.DMA
    vmem = pl.BlockSpec(memory_space=pltpu.VMEM)
    return pl.pallas_call(
        functools.partial(fused_kernel, dims, factor),
        out_shape=(
            jax.ShapeDtypeStruct((tok, I * depth), BF16),
            jax.ShapeDtypeStruct((rows, width), F32),
            jax.ShapeDtypeStruct((rows, width), F32),
        ),
        in_specs=[vmem] * 9,
        out_specs=(vmem, vmem, vmem),
        scratch_shapes=[
            pltpu.VMEM((NC, 2, I, slab, CW), BF16),
            pltpu.VMEM((NC, 2, Z, rows, CW), BF16),
            pltpu.VMEM((NC, Z, 2, rows, CW), BF16),
            pltpu.VMEM((NC, Z + 1, 2, rows, CW), BF16),
            pltpu.VMEM((depth, S * tok), BF16),
            pltpu.VMEM((slab, depth), F32),
            pltpu.VMEM((S, tok, depth), BF16),
            pltpu.VMEM((S, tok, depth), BF16),
            pltpu.VMEM((tok, I * depth), F32),
            dma((NC, 2, Z)),
            dma((NC, Z)),
            dma((NC, Z)),
            dma((NC, Z + 1)),
            dma((NC, X)),
            dma((NC, X)),
            dma((NC, X)),
            dma((NC, X)),
            dma((S,)),
            dma((S,)),
            dma((S,)),
            dma((S,)),
        ],
        compiler_params=pltpu.CompilerParams(
            collective_id=0, has_side_effects=True, vmem_limit_bytes=61 * 1024 * 1024
        ),
        cost_estimate=pl.CostEstimate(
            flops=8 * slab * I * depth * width, bytes_accessed=20 * 1024 * 1024, transcendentals=slab * width
        ),
    )(normed, gate_pre, up_pre, hidden_grad, gate_weight, up_weight, unit_rows, inverse, gain)


def body(
    quant_rows,
    residual,
    row_scale,
    norm_gain,
    gate_pre,
    up_pre,
    hidden_grad,
    gate_weight,
    up_weight,
):
    count = lax.axis_size("dp")
    tensor = lax.axis_size("tensor")
    Z = line_length(count)
    I = count // Z
    tok, depth = residual.shape
    rows = gate_weight.shape[0]
    NC = chunk_count(gate_weight.shape[1])
    CW = gate_weight.shape[1] // NC
    summed_in = residual.astype(F32) + quant_rows.astype(F32) * row_scale[:, None]
    inverse = lax.rsqrt(jnp.mean(summed_in * summed_in, axis=-1, keepdims=True) + 1e-05)
    unit_rows = summed_in * inverse
    normed = (unit_rows * norm_gain).astype(BF16)
    blocks = normed.reshape(tok, Z, I, rows).transpose(2, 1, 3, 0).reshape(I, Z * rows, tok)
    factor = 1.0 / math.sqrt(gate_pre.shape[0] * count)
    return fused(
        (Z, I, tensor, NC, CW), factor, blocks, gate_pre, up_pre, hidden_grad, gate_weight, up_weight,
        unit_rows, inverse, norm_gain[None, :],
    )


def solution(mesh):
    placed = (
        P(("dp", "tensor"), None),
        P(("dp", "tensor"), None),
        P(("dp", "tensor")),
        P(),
        P("dp", "tensor"),
        P("dp", "tensor"),
        P("dp", "tensor"),
        P("dp", "tensor"),
        P("dp", "tensor"),
    )
    return jax.shard_map(
        body,
        mesh=mesh,
        in_specs=placed,
        out_specs=(P(("dp", "tensor"), None), P("dp", "tensor"), P("dp", "tensor")),
        check_vma=False,
    )
```

```python
import functools
import math

import jax
import jax.numpy as jnp
from jax import lax
from jax.experimental import pallas as pl
from jax.experimental.pallas import tpu as pltpu
from jax.sharding import PartitionSpec as P

MESH = pl.DeviceIdType.MESH
BF16 = jnp.bfloat16
F32 = jnp.float32
CORES = 2


def line_length(dp):
    for length in (4, 2):
        if dp % (length * CORES) == 0:
            return length
    return 1


def chunk_count(width):
    for count in (7, 4, 2):
        if width % (count * 128) == 0:
            return count
    return 1


def fused_kernel(
    dims,
    factor,
    quant_ref,
    residual_ref,
    scale_ref,
    gate_ref,
    up_ref,
    hidden_ref,
    gate_w_ref,
    up_w_ref,
    gain_ref,
    grad_out,
    gate_out,
    up_out,
    acts,
    weights,
    rs_send,
    rs_recv,
    normed_all,
    acc,
    ng_send,
    ng_recv,
    terms,
    unit_ref,
    inverse_ref,
    normed_ref,
    ag_ss,
    ag_rs,
    rs_ss,
    rs_rs,
    gx_ss,
    gx_rs,
    gc_ss,
    gc_rs,
    n_ss,
    n_rs,
    ng_ss,
    ng_rs,
):
    Z, I, NT, NC, CW = dims
    X = I // CORES
    S = I * NT
    slab = gate_ref.shape[0]
    rows = gate_w_ref.shape[0]
    tok = slab // NT
    dp = lax.axis_index("dp")
    y = lax.axis_index("tensor")
    z = lax.div(dp, I)
    i = lax.rem(dp, I)
    x = lax.div(i, CORES)
    c = lax.rem(i, CORES)
    me = i * NT + y
    base = z * I
    partner = (base + x * CORES + (1 - c), y)
    right = (dp + I, y)
    left = (dp - I, y)

    def member(s):
        return (base + lax.div(s, NT), lax.rem(s, NT))

    def across(other):
        return (base + other * CORES + c, y)

    def copy(src, dst, send_sem, recv_sem, device):
        return pltpu.make_async_remote_copy(
            src_ref=src, dst_ref=dst, send_sem=send_sem, recv_sem=recv_sem,
            device_id=device, device_id_type=MESH,
        )

    barrier = pltpu.get_barrier_semaphore()

    @pl.loop(0, S)
    def _(s):
        @pl.when(s != me)
        def _():
            pl.semaphore_signal(barrier, inc=1, device_id=member(s), device_id_type=MESH)

    @pl.when(z < Z - 1)
    def _():
        pl.semaphore_signal(barrier, inc=1, device_id=right, device_id_type=MESH)

    @pl.when(z > 0)
    def _():
        pl.semaphore_signal(barrier, inc=1, device_id=left, device_id_type=MESH)

    @pl.loop(0, NC)
    def _(k):
        columns = pl.ds(pl.multiple_of(k * CW, 128), CW)
        weights[k, 0, z] = gate_w_ref[:, columns]
        weights[k, 1, z] = up_w_ref[:, columns]

    inside = (z > 0) & (z < Z - 1)

    @pl.when(inside)
    def _():
        pl.semaphore_wait(barrier, S + 1)

    @pl.when(jnp.logical_not(inside))
    def _():
        pl.semaphore_wait(barrier, S if Z > 1 else S - 1)

    def ag_right(k, origin):
        block = weights.at[k, :, origin]
        return copy(block, block, ag_ss.at[k, 0, origin], ag_rs.at[k, origin], right)

    def ag_left(k, origin):
        block = weights.at[k, :, origin]
        return copy(block, block, ag_ss.at[k, 1, origin], ag_rs.at[k, origin], left)

    def normed_copy(s, source):
        place = pl.ds(pl.multiple_of(source * tok, 128), tok)
        return copy(
            normed_ref.at[lax.div(s, NT)], normed_all.at[:, place], n_ss.at[s], n_rs.at[source], member(s)
        )

    @pl.loop(0, NC)
    def _(k):
        @pl.when(z < Z - 1)
        def _():
            ag_right(k, z).start()

        @pl.when(z > 0)
        def _():
            ag_left(k, z).start()

    summed_in = residual_ref[...].astype(F32) + quant_ref[...].astype(F32) * scale_ref[...]
    inverse = lax.rsqrt(jnp.mean(summed_in * summed_in, axis=-1, keepdims=True) + 1e-05)
    inverse_ref[...] = inverse
    unit_ref[...] = summed_in * inverse
    for j in range(I):
        for o in range(Z):
            first = (o * I + j) * rows
            scaled_rows = unit_ref[:, first : first + rows] * gain_ref[:, first : first + rows]
            normed_ref[j, o * rows : (o + 1) * rows] = scaled_rows.T.astype(BF16)

    @pl.loop(0, S)
    def _(s):
        @pl.when(s != me)
        def _():
            normed_copy(s, me).start()

    normed_all[:, pl.ds(pl.multiple_of(me * tok, 128), tok)] = normed_ref[i]

    def act_across(k, other, source):
        block = acts.at[k, :, source * CORES + c]
        return copy(block, block, gx_ss.at[k, other], gx_rs.at[k, source], across(other))

    def act_partner(k, source_x, source_c):
        block = acts.at[k, :, source_x * CORES + source_c]
        return copy(block, block, gc_ss.at[k, source_x], gc_rs.at[k, source_x], partner)

    part = 32

    @pl.loop(0, NC)
    def _(k):
        columns = pl.ds(pl.multiple_of(k * CW, 128), CW)

        @pl.loop(0, slab // part)
        def _(r):
            span = pl.ds(pl.multiple_of(r * part, part), part)
            gate_val = gate_ref[span, columns].astype(F32)
            up_val = up_ref[span, columns].astype(F32)
            grad_val = hidden_ref[span, columns].astype(F32)
            sig = 1.0 / (1.0 + jnp.exp(-gate_val))
            scaled = grad_val * sig
            acts[k, 1, i, span] = (scaled * gate_val).astype(BF16)
            acts[k, 0, i, span] = (scaled * up_val * (1.0 + gate_val * (1.0 - sig))).astype(BF16)

        @pl.loop(0, X)
        def _(other):
            @pl.when(other != x)
            def _():
                act_across(k, other, x).start()

        act_partner(k, x, c).start()

    def rs_right(k, d):
        return copy(rs_send.at[k, d], rs_recv.at[k, d], rs_ss.at[k, d], rs_rs.at[k, d], right)

    def rs_left(k, d, slot):
        return copy(rs_send.at[k, d], rs_recv.at[k, slot], rs_ss.at[k, d], rs_rs.at[k, slot], left)

    def add_in(k, d):
        for t in range(2):
            rs_send[k, d, t] = (rs_send[k, d, t].astype(F32) + rs_recv[k, d, t].astype(F32)).astype(BF16)

    @pl.loop(0, S)
    def _(s):
        @pl.when(s != me)
        def _():
            normed_copy(s, s).wait_recv()

    @pl.loop(0, NC + max(Z - 2, 0))
    def _(it):
        for h in range(1, Z - 1):
            kh = it - h

            @pl.when((kh >= 0) & (kh < NC) & (z >= h) & (z < Z - 1))
            def _():
                ag_right(kh, z - h).wait_recv()
                ag_right(kh, z - h).start()

            @pl.when((kh >= 0) & (kh < NC) & (z + h < Z) & (z > 0))
            def _():
                ag_left(kh, z + h).wait_recv()
                ag_left(kh, z + h).start()

        @pl.when(it < NC)
        def _():
            @pl.loop(0, X)
            def _(other):
                @pl.when(other != x)
                def _():
                    act_across(it, other, other).wait_recv()
                    act_partner(it, other, c).start()

            @pl.loop(0, X)
            def _(other):
                act_partner(it, other, 1 - c).wait_recv()

            for t in range(2):
                full = jnp.zeros((Z * rows, CW), F32)
                for j in range(I):
                    full = full + jnp.dot(
                        normed_all[:, j * slab : (j + 1) * slab], acts[it, t, j],
                        preferred_element_type=F32,
                    )
                for d in range(Z):
                    rs_send[it, d, t] = full[d * rows : (d + 1) * rows].astype(BF16)

            @pl.when((z == 0) & (Z > 1))
            def _():
                for d in range(Z - 1, 0, -1):
                    rs_right(it, d).start()

            @pl.when((z == Z - 1) & (Z > 1))
            def _():
                for d in range(Z - 1):
                    rs_left(it, d, d if d < Z - 2 else Z).start()

    def ng_copy(s, source):
        return copy(ng_send.at[s], ng_recv.at[source], ng_ss.at[s], ng_rs.at[source], member(s))

    def weights_there():
        @pl.loop(0, NC)
        def _(k):
            for o in range(Z):
                @pl.when((z == Z - 1) & (z != o))
                def _():
                    ag_left(k, o).wait_recv()

                @pl.when((z == 0) & (z != o))
                def _():
                    ag_right(k, o).wait_recv()

    def normed_gradient(j):
        acc[...] = jnp.zeros_like(acc)

        @pl.loop(0, NC)
        def _(k):
            for t in range(2):
                acc[...] += lax.dot_general(
                    acts[k, t, j], weights[k, t].reshape(Z * rows, CW),
                    (((1,), (1,)), ((), ())), preferred_element_type=F32,
                )

        @pl.loop(0, NT)
        def _(h):
            s = j * NT + h
            ng_send[s] = acc[pl.ds(pl.multiple_of(h * tok, 128), tok), :].astype(BF16)

            @pl.when(s != me)
            def _():
                ng_copy(s, me).start()

    weights_there()

    @pl.loop(0, max(NC + max(Z - 3, 0), I + 1))
    def _(it):
        kr = it - jnp.maximum(z - 1, 0)

        @pl.when((kr >= 0) & (kr < NC) & (z > 0) & (z < Z - 1))
        def _():
            for d in range(Z - 1, 1, -1):
                @pl.when(d > z)
                def _():
                    rs_right(kr, d).wait_recv()
                    add_in(kr, d)
                    rs_right(kr, d).start()

        kl = it - jnp.maximum(Z - 2 - z, 0)

        @pl.when((kl >= 0) & (kl < NC) & (z > 0) & (z < Z - 1))
        def _():
            for d in range(Z - 2):
                @pl.when(d < z)
                def _():
                    rs_left(kl, d, d).wait_recv()
                    add_in(kl, d)

                    @pl.when(d < z - 1)
                    def _():
                        rs_left(kl, d, d).start()

                    @pl.when(d == z - 1)
                    def _():
                        rs_left(kl, d, Z).start()

        @pl.when((it >= 1) & (it < I + 1))
        def _():
            normed_gradient(it - 1)

    ng_recv[me] = ng_send[me]

    @pl.loop(0, S)
    def _(s):
        @pl.when(s != me)
        def _():
            ng_copy(s, s).wait_recv()

    tally = jnp.zeros((tok, 1), F32)
    for j in range(I):
        total = ng_recv[j * NT].astype(F32)
        for h in range(1, NT):
            total = total + ng_recv[j * NT + h].astype(F32)
        for o in range(Z):
            first = (o * I + j) * rows
            term = gain_ref[:, first : first + rows] * total[:, o * rows : (o + 1) * rows]
            terms[:, first : first + rows] = term
            tally = tally + jnp.sum(unit_ref[:, first : first + rows] * term, axis=-1, keepdims=True)
    mean = tally * (1.0 / (I * Z * rows))
    grad_out[...] = (inverse_ref[...] * (terms[...] - unit_ref[...] * mean)).astype(BF16)

    @pl.loop(0, NC)
    def _(k):
        columns = pl.ds(pl.multiple_of(k * CW, 128), CW)
        gate_out[:, columns] = rs_send[k, z, 0].astype(F32) * factor
        up_out[:, columns] = rs_send[k, z, 1].astype(F32) * factor

        @pl.when(z > 0)
        def _():
            rs_right(k, z).wait_recv()
            gate_out[:, columns] += rs_recv[k, z, 0].astype(F32) * factor
            up_out[:, columns] += rs_recv[k, z, 1].astype(F32) * factor

        @pl.when(z < Z - 1)
        def _():
            rs_left(k, z, Z).wait_recv()
            gate_out[:, columns] += rs_recv[k, Z, 0].astype(F32) * factor
            up_out[:, columns] += rs_recv[k, Z, 1].astype(F32) * factor

    @pl.loop(0, S)
    def _(s):
        @pl.when(s != me)
        def _():
            normed_copy(s, me).wait_send()
            ng_copy(s, me).wait_send()

    @pl.loop(0, NC)
    def _(k):
        @pl.loop(0, X)
        def _(other):
            act_partner(k, other, c).wait_send()

            @pl.when(other != x)
            def _():
                act_across(k, other, x).wait_send()

        for d in range(Z):
            @pl.when(d > z)
            def _():
                rs_right(k, d).wait_send()

            @pl.when(d < z)
            def _():
                rs_left(k, d, d).wait_send()

            @pl.when((z < Z - 1) & (d <= z))
            def _():
                ag_right(k, d).wait_send()

            @pl.when((z > 0) & (d >= z))
            def _():
                ag_left(k, d).wait_send()


def fused(dims, factor, quant_rows, residual, scale, gate_pre, up_pre, hidden_grad, gate_weight, up_weight, gain):
    Z, I, NT, NC, CW = dims
    X = I // CORES
    S = I * NT
    slab = gate_pre.shape[0]
    rows, width = gate_weight.shape
    tok = slab // NT
    depth = Z * rows
    dma = pltpu.SemaphoreType.DMA
    vmem = pl.BlockSpec(memory_space=pltpu.VMEM)
    return pl.pallas_call(
        functools.partial(fused_kernel, dims, factor),
        out_shape=(
            jax.ShapeDtypeStruct((tok, I * depth), BF16),
            jax.ShapeDtypeStruct((rows, width), F32),
            jax.ShapeDtypeStruct((rows, width), F32),
        ),
        in_specs=[vmem] * 9,
        out_specs=(vmem, vmem, vmem),
        scratch_shapes=[
            pltpu.VMEM((NC, 2, I, slab, CW), BF16),
            pltpu.VMEM((NC, 2, Z, rows, CW), BF16),
            pltpu.VMEM((NC, Z, 2, rows, CW), BF16),
            pltpu.VMEM((NC, Z + 1, 2, rows, CW), BF16),
            pltpu.VMEM((depth, S * tok), BF16),
            pltpu.VMEM((slab, depth), F32),
            pltpu.VMEM((S, tok, depth), BF16),
            pltpu.VMEM((S, tok, depth), BF16),
            pltpu.VMEM((tok, I * depth), F32),
            pltpu.VMEM((tok, I * depth), F32),
            pltpu.VMEM((tok, 1), F32),
            pltpu.VMEM((I, depth, tok), BF16),
            dma((NC, 2, Z)),
            dma((NC, Z)),
            dma((NC, Z)),
            dma((NC, Z + 1)),
            dma((NC, X)),
            dma((NC, X)),
            dma((NC, X)),
            dma((NC, X)),
            dma((S,)),
            dma((S,)),
            dma((S,)),
            dma((S,)),
        ],
        compiler_params=pltpu.CompilerParams(
            collective_id=0, has_side_effects=True, vmem_limit_bytes=61 * 1024 * 1024
        ),
        cost_estimate=pl.CostEstimate(
            flops=8 * slab * I * depth * width, bytes_accessed=20 * 1024 * 1024, transcendentals=slab * width
        ),
    )(quant_rows, residual, scale, gate_pre, up_pre, hidden_grad, gate_weight, up_weight, gain)


def body(
    quant_rows,
    residual,
    row_scale,
    norm_gain,
    gate_pre,
    up_pre,
    hidden_grad,
    gate_weight,
    up_weight,
):
    count = lax.axis_size("dp")
    tensor = lax.axis_size("tensor")
    Z = line_length(count)
    I = count // Z
    NC = chunk_count(gate_weight.shape[1])
    CW = gate_weight.shape[1] // NC
    factor = 1.0 / math.sqrt(gate_pre.shape[0] * count)
    return fused(
        (Z, I, tensor, NC, CW), factor, quant_rows, residual, row_scale[:, None],
        gate_pre, up_pre, hidden_grad, gate_weight, up_weight, norm_gain[None, :],
    )


def solution(mesh):
    placed = (
        P(("dp", "tensor"), None),
        P(("dp", "tensor"), None),
        P(("dp", "tensor")),
        P(),
        P("dp", "tensor"),
        P("dp", "tensor"),
        P("dp", "tensor"),
        P("dp", "tensor"),
        P("dp", "tensor"),
    )
    return jax.shard_map(
        body,
        mesh=mesh,
        in_specs=placed,
        out_specs=(P(("dp", "tensor"), None), P("dp", "tensor"), P("dp", "tensor")),
        check_vma=False,
    )
```
